128 devices in a mesh: inner: 16 (over z, y), target: 8 (over x, core).
Axes of the slice: x: 4, y: 4, z: 4, core: 2. Of those that a mesh axis runs over, the one named last changes fastest.
Arguments:
- left_factors: float32 [64, 64, 1024, 64], P('target', 'inner'), may hold values from -6 to 6
- mid_factors: float32 [64, 64, 1024, 64], P('target', 'inner'), may hold values from -0.1875 to 0.1875
- row_factors: float32 [64, 1024, 64], P('inner'), may hold values from -6 to 6
- col_factors: float32 [64, 1024, 64], P('inner'), may hold values from -0.09375 to 0.09375
- lists: int32 [64, 64], P('target'), may hold values from -1 to 63, as said below
- sketch_right: float32 [1024, 128], replicated, may hold values from -0.046875 to 0.046875
- sketch_left: float32 [1024, 128], replicated, may hold values from -0.046875 to 0.046875
- diag_tile: float32 [1024, 1024], P(None, 'target'), as said below
Outputs:
- left_sketch: float32 [64, 1024, 128], P('target', 'inner')
- right_factor: float32 [64, 128, 1024], P('target', 'inner')
- core: float32 [64, 128, 128], P('target', 'inner')
The draws below stay inside these ranges and needn't reach their ends.
Inputs may be any that keep to these rules, and one draw needn't show every extreme that they name: `lists`: row t holds each contributing inner index once in any order and -1 in the other slots; the contributing indices of a row are 0 to c - 1 for some count c of 1 to 64, and some row has all 64. `diag_tile`: upper triangular with diagonal entries of 1 to 2.
All inputs are finite; a program needn't handle non-finite values.
Results may differ from the reference program's by a relative error of at most 0.0003.
Values sent between devices are 32-bit elements; how exact they have to be, the bound alone decides.
A program may use at most 128 MiB of HBM per device.

```python
import jax
import jax.numpy as jnp
from jax import lax

B = 1024
R = 64
S = 128
TGT = 64
INNER = 64


def draw_lists(key, part):
    count_key, pick_key, perm_key = jax.random.split(jax.random.fold_in(key, 17), 3)
    counts = jax.random.randint(count_key, (TGT,), 1, INNER + 1)
    chosen = jax.random.randint(pick_key, (), 0, TGT)
    counts = jnp.where(jnp.arange(TGT) == chosen, INNER, counts)
    perm_keys = jax.random.split(perm_key, TGT)
    orders = jax.vmap(lambda k: jax.random.permutation(k, INNER))(perm_keys).astype(jnp.int32)
    return jnp.where(orders < counts[:, None], orders, -1).astype(jnp.int32)


def draw_diag_tile(key, part):
    off_key, dia_key = jax.random.split(jax.random.fold_in(key, 29))
    upper = jax.random.normal(off_key, (B, B), jnp.float32) * 0.6 * (1.0 / B) ** 0.5
    diagonal = jax.random.uniform(dia_key, (B,), jnp.float32, 1.0, 2.0)
    return (jnp.triu(upper, 1) + jnp.diag(diagonal)).astype(jnp.float32)


def block_scale(rng, dims, cuts, smallest, largest):
    level, own = 1.0, jax.random.fold_in(rng, 6)
    for dim, blocks in cuts:
        draws = jnp.exp(jax.random.uniform(jax.random.fold_in(own, dim), (blocks,), jnp.float32, smallest / len(cuts), largest / len(cuts)))
        level = level * jnp.repeat(draws, dims[dim] // blocks).reshape([-1 if axis == dim else 1 for axis in range(len(dims))])
    return level


def noise(stream_key, shape, deviation, reach, cuts=(), kind=jnp.bfloat16):
    loudness = block_scale(stream_key, shape, cuts, -0.22, 0.18) if cuts else 1.0
    values = jax.random.normal(stream_key, shape, jnp.float32) * deviation * loudness
    return jnp.minimum(jnp.maximum(values, -reach), reach).astype(kind)


def setup_inputs(seed: int = 0) -> dict:
    key_of = jax.random.split(jax.random.key(seed), 9)
    return {
        "left_factors": noise(key_of[0], (TGT, INNER, B, R), 1.0, 6.0, ((0, 8), (1, 16)), jnp.float32),
        "mid_factors": noise(key_of[1], (TGT, INNER, B, R), B ** -0.5, 0.1875, ((0, 8), (1, 16)), jnp.float32),
        "row_factors": noise(key_of[2], (INNER, B, R), 1.0, 6.0, ((0, 16),), jnp.float32),
        "col_factors": noise(key_of[3], (INNER, B, R), (64 * R) ** -0.5, 0.09375, ((0, 16),), jnp.float32),
        "lists": draw_lists(jax.random.fold_in(key_of[8], 71), 0),
        "sketch_right": noise(key_of[5], (B, S), (16 * B) ** -0.5, 0.046875, (), jnp.float32),
        "sketch_left": noise(key_of[6], (B, S), (16 * B) ** -0.5, 0.046875, (), jnp.float32),
        "diag_tile": draw_diag_tile(jax.random.fold_in(key_of[8], 71), 0),
    }


precision_top = lax.Precision.HIGHEST

def reference(left_factors, mid_factors, row_factors, col_factors, lists, sketch_right, sketch_left, diag_tile):
    inner_ids = jnp.arange(INNER, dtype=jnp.int32)
    col_sketch = jnp.einsum('kbr,bs->krs', col_factors, sketch_right, precision=precision_top)

    def one_target(items):
        left_tile, mid_tile, row_list = items
        present = jnp.sum((row_list[:, None] == inner_ids[None, :]).astype(jnp.float32), axis=0)
        coupling = jnp.einsum('kbr,kbq->krq', mid_tile, row_factors, precision=precision_top) * present[:, None, None]
        inner_left = jnp.einsum('krq,kqs->krs', coupling, col_sketch, precision=precision_top)
        left_out = jnp.einsum('kbr,krs->bs', left_tile, inner_left, precision=precision_top)
        projected = jnp.einsum('bs,kbr->ksr', sketch_left, left_tile, precision=precision_top)
        joined = jnp.einsum('ksr,krq->ksq', projected, coupling, precision=precision_top)
        right_sketch = jnp.einsum('ksq,kbq->sb', joined, col_factors, precision=precision_top)
        core_out = jnp.dot(right_sketch, sketch_right, precision=precision_top)
        solved = lax.linalg.triangular_solve(diag_tile, right_sketch, left_side=False, lower=False)
        return (left_out, solved, core_out)
    return lax.map(one_target, (left_factors, mid_factors, lists))
```

```python
import functools

import jax
import jax.numpy as jnp
from jax import lax
from jax.experimental import pallas as pl
from jax.experimental.pallas import tpu as pltpu
from jax.sharding import PartitionSpec as P

F32 = jnp.float32
BF16 = jnp.bfloat16
MESH = pl.DeviceIdType.MESH
NN = ((1,), (0,))
NT = ((1,), (1,))
SIDE = 4
UNITS = 16


def split(value):
    high = value.astype(BF16)
    return high, (value - high.astype(F32)).astype(BF16)


def mm(a, b, dims):
    return lax.dot_general(a, b, (dims, ((), ())), preferred_element_type=F32)


def mm3(a, b, dims):
    return mm(a[0], b[0], dims) + (mm(a[1], b[0], dims) + mm(a[0], b[1], dims))


def mm_top(a, b):
    return lax.dot_general(
        a, b, (NN, ((), ())), precision=lax.Precision.HIGHEST, preferred_element_type=F32
    )


def kernel(
    lt_hbm, mt_hbm, rt_hbm, ct_hbm, lists, om_hbm, psi_hbm, d_hbm,
    left_out, rf_out, core_out,
    lt, mt, rt, ct, om, psi, dfull, dinv, part, half, far1, near1, far2, near2,
    rts, psts, cols, ms, ls, cs, js, ws, doms,
    in_sem, send_sem, recv_sem, gs_sem, gr_sem,
):
    inner = lax.axis_index("inner")
    target = lax.axis_index("target")
    z, y = inner // SIDE, lax.rem(inner, SIDE)
    x, core = target // 2, lax.rem(target, 2)

    def turn(v, step):
        return lax.rem(v + step, SIDE)

    z_next = (turn(z, 1) * SIDE + y, turn(z, 3) * SIDE + y)
    y_next = (z * SIDE + turn(y, 1), z * SIDE + turn(y, 3))
    x_next = (turn(x, 1) * 2 + core, turn(x, 3) * 2 + core)
    sibling = x * 2 + (1 - core)

    loads = []

    def load(src, dst):
        copy = pltpu.make_async_copy(src, dst, in_sem.at[len(loads)])
        copy.start()
        loads.append(copy)
        return copy

    rt_load = load(rt_hbm, rt)
    ct_load = load(ct_hbm, ct)
    om_load = load(om_hbm, om)
    d_load = load(d_hbm, dfull.at[target])
    psi_load = load(psi_hbm, psi)
    in_base = 8

    def mt_copy(t):
        return pltpu.make_async_copy(mt_hbm.at[t], mt.at[t], in_sem.at[in_base + t])

    def lt_copy(t):
        return pltpu.make_async_copy(lt_hbm.at[t], lt.at[t], in_sem.at[in_base + 8 + t])

    @pl.loop(0, 8)
    def _(t):
        mt_copy(t).start()
        lt_copy(t).start()

    barrier = pltpu.get_barrier_semaphore()
    for peer in z_next + y_next:
        pl.semaphore_signal(barrier, inc=1, device_id=(peer, target), device_id_type=MESH)
    for peer in x_next + (sibling,):
        pl.semaphore_signal(barrier, inc=1, device_id=(inner, peer), device_id_type=MESH)
    pl.semaphore_wait(barrier, 7)

    def g_copy(src, dst, sem, peer):
        return pltpu.make_async_remote_copy(
            src_ref=src, dst_ref=dst, send_sem=gs_sem.at[sem], recv_sem=gr_sem.at[sem],
            device_id=(inner, peer), device_id_type=MESH,
        )

    def x_at(step, which):
        return turn(x, step) * 2 + which

    def gather_first(src, dst, base):
        for sem, peer in ((0, x_next[0]), (1, x_next[1]), (4, sibling)):
            g_copy(src, dst.at[target], base + sem, peer).start()

    def gather_second(dst, base, rows):
        before, after = dst.at[x_at(3, core)], dst.at[x_at(1, core)]
        g_copy(before, before, base + 0, sibling).wait_recv()
        g_copy(after, after, base + 1, sibling).wait_recv()
        low, top = before.at[pl.ds(0, rows)], after.at[pl.ds(rows, rows)]
        g_copy(low, low, base + 2, x_next[0]).start()
        g_copy(top, top, base + 3, x_next[1]).start()
        g_copy(before, before, base + 5, sibling).start()
        g_copy(after, after, base + 6, sibling).start()

    def gather_third(dst, base, rows):
        away = dst.at[x_at(2, core)]
        low, top = away.at[pl.ds(0, rows)], away.at[pl.ds(rows, rows)]
        g_copy(low, low, base + 2, sibling).wait_recv()
        g_copy(top, top, base + 3, sibling).wait_recv()
        g_copy(away, away, base + 7, sibling).start()

    def gather_last(dst, base):
        for sem, step in ((4, 0), (5, 3), (6, 1), (7, 2)):
            block = dst.at[x_at(step, 1 - core)]
            g_copy(block, block, base + sem, sibling).wait_recv()

    def gather_sent(src, dst, base, rows):
        for sem in (0, 1, 4, 5, 6, 7):
            g_copy(dst.at[0], dst.at[0], base + sem, sibling).wait_send()
        for sem in (2, 3):
            piece = dst.at[0, pl.ds(0, rows)]
            g_copy(piece, piece, base + sem, sibling).wait_send()

    gather_first(d_hbm, dfull, 0)

    def place(u, stage):
        axis = lax.rem(u + stage, 2)
        pos = z + axis * (y - z)
        peers = tuple(a + axis * (b - a) for a, b in zip(z_next, y_next))
        return pos, peers

    bufs = ((part, far1, near1, 2), (half, far2, near2, 1))

    def r_copy(stage, u, sem, src, dst, peer):
        return pltpu.make_async_remote_copy(
            src_ref=src, dst_ref=dst,
            send_sem=send_sem.at[stage, u, sem], recv_sem=recv_sem.at[stage, u, sem],
            device_id=(peer, target), device_id_type=MESH,
        )

    def piece(stage, u, chunk, h):
        buf, _, _, w = bufs[stage]
        return buf.at[u, pl.ds((2 * chunk + h) * w, w)]

    def start(stage, u):
        pos, peers = place(u, stage)
        _, far, near, _ = bufs[stage]
        for d in (0, 1):
            r_copy(stage, u, d, piece(stage, u, turn(pos, 2), d), far.at[u, d], peers[d]).start()
        for d in (0, 1):
            r_copy(
                stage, u, 2 + d, piece(stage, u, turn(pos, 1 + 2 * d), 1 - d),
                near.at[u, d, 1 - d], peers[d],
            ).start()

    def middle(stage, u):
        pos, peers = place(u, stage)
        _, far, near, _ = bufs[stage]
        for d in (0, 1):
            own = piece(stage, u, turn(pos, 1 + 2 * d), d)
            r_copy(stage, u, d, far.at[u, d], far.at[u, d], peers[d]).wait_recv()
            own[...] += far[u, d]
            r_copy(stage, u, 4 + d, own, near.at[u, d, d], peers[d]).start()

    def finish(stage, u):
        pos, peers = place(u, stage)
        _, far, near, _ = bufs[stage]
        for d in (0, 1):
            for h in (0, 1):
                sem = 4 + d if h == d else 2 + d
                r_copy(stage, u, sem, near.at[u, d, h], near.at[u, d, h], peers[d]).wait_recv()
        return [
            piece(stage, u, pos, h)[...] + near[u, 0, h] + near[u, 1, h] for h in (0, 1)
        ]

    def sent(stage, u):
        _, far, _, _ = bufs[stage]
        for sem in range(6):
            r_copy(stage, u, sem, far.at[u, 0], far.at[u, 0], z_next[0]).wait_send()

    def finish_first(u):
        for h, value in enumerate(finish(0, u)):
            half[u, pl.ds(4 * h, 4)] = value.reshape(4, 32, 128)
        start(1, u)

    def finish_second(u):
        values = [v.reshape(32, 128) for v in finish(1, u)]

        @pl.when(u < 8)
        def _():
            for h in (0, 1):
                left_out[u, pl.ds(32 * h, 32), :] = values[h]

        @pl.when(u >= 8)
        def _():
            for h in (0, 1):
                for m in range(4):
                    rf_out[u - 8, :, pl.ds((4 * h + m) * 128, 128)] = values[h][
                        8 * m : 8 * m + 8
                    ]

    def within(s):
        return jnp.logical_and(s >= 0, s < UNITS)

    def service(s):
        pl.when(within(s - 1))(lambda: middle(0, s - 1))
        pl.when(within(s - 2))(lambda: finish_first(s - 2))
        pl.when(within(s - 3))(lambda: middle(1, s - 3))
        pl.when(within(s - 4))(lambda: finish_second(s - 4))

    def chunk_at(u, zz, yy):
        axis = lax.rem(u, 2)
        first, second = zz + axis * (yy - zz), yy + axis * (zz - yy)
        return first * SIDE + second

    def put(ref, value):
        ref[0], ref[1] = split(value)

    def got(ref):
        return ref[0], ref[1]

    rt_load.wait()
    put(rts, rt[...])
    ct_load.wait()
    om_load.wait()
    put(cols, mm3(split(ct[...]), split(om[...]), NN).T)

    row_tile = lax.broadcasted_iota(jnp.int32, (256, 256), 0) // 64
    col_tile = lax.broadcasted_iota(jnp.int32, (256, 256), 1) // 64
    tile_ids = inner * 4 + lax.broadcasted_iota(jnp.int32, (256, 1), 0) // 64

    def left_unit(t):
        mt_copy(t).wait()
        put(ms, mt[t])
        coupling = mm3(got(ms), got(rts), NT)
        present = jnp.sum(
            (lists[pl.ds(t, 1), :] == tile_ids).astype(F32), axis=1, keepdims=True
        )
        coupling = jnp.where(row_tile == col_tile, coupling, 0.0) * present
        put(cs, coupling)
        inner_left = split(mm3(got(cols), got(cs), NT))
        lt_copy(t).wait()
        put(ls, lt[t])
        for zz in range(4):
            cut = pl.ds(256 * zz, 256)
            block = mm3(inner_left, (ls[0, :, cut], ls[1, :, cut]), NN).T
            for yy in range(4):
                part[t, chunk_at(t, zz, yy)] = block[64 * yy : 64 * yy + 64]
        start(0, t)
        projected = split(mm3(got(psts), got(ls), NT))
        put(js.at[t], mm3(projected, got(cs), NN))

    def right_unit(t):
        u = t + 8
        for n in range(4):
            cut = pl.ds(256 * n, 256)
            block = mm3(got(js.at[t]), (ws[0, :, cut], ws[1, :, cut]), NN)
            for m in (0, 1):
                value = block[:, 128 * m : 128 * m + 128].reshape(16, 8, 128)
                for i in range(16):
                    part[u, chunk_at(u, i // 4, i % 4), pl.ds((2 * n + m) * 8, 8), :] = value[i]
        start(0, u)

    def own_inverse():
        d_load.wait()
        block = dfull[target, pl.ds(pl.multiple_of(target * 128, 128), 128), :]
        rows = lax.broadcasted_iota(jnp.int32, (128, 128), 0)
        lanes = lax.broadcasted_iota(jnp.int32, (128, 128), 1)
        eye = (rows == lanes).astype(F32)
        diagonal = jnp.where(rows == lanes, block, 0.0)
        power = eye - block / jnp.sum(diagonal, axis=1, keepdims=True)
        product = eye + power
        for _ in range(6):
            power = mm_top(power, power)
            product = product + mm_top(product, power)
        dinv[target] = product / jnp.sum(diagonal, axis=0, keepdims=True)

    def solve_columns():
        for j in range(8):
            cut = pl.ds(128 * j, 128)
            rhs = ct[:, cut]
            if j > 0:
                before = pl.ds(0, 128 * j)
                rhs = rhs - mm3(
                    (ws[0, :, before], ws[1, :, before]), split(dfull[j, before, :]), NN
                )
            ws[0, :, cut], ws[1, :, cut] = split(mm3(split(rhs), split(dinv[j]), NN))

    psi_load.wait()
    put(psts, psi[...].T)

    @pl.loop(0, 8)
    def _(s):
        left_unit(s)

        @pl.when(s == 1)
        def _():
            own_inverse()
            gather_first(dinv.at[target], dinv, 8)

        @pl.when(s == 4)
        def _():
            gather_second(dfull, 0, 512)
            gather_second(dinv, 8, 64)

        @pl.when(s == 6)
        def _():
            gather_third(dfull, 0, 512)
            gather_third(dinv, 8, 64)

        service(s)

    gather_last(dfull, 0)
    gather_last(dinv, 8)
    solve_columns()

    @pl.loop(8, 16)
    def _(s):
        right_unit(s - 8)
        service(s)

    omega = split(om[...])
    for i in range(8):
        acc = jnp.zeros((128, 128), F32)
        for j in range(i, 8):
            acc += mm3(
                split(dfull[j, pl.ds(128 * i, 128), :]),
                (omega[0][128 * j : 128 * j + 128], omega[1][128 * j : 128 * j + 128]),
                NN,
            )
        doms[0, pl.ds(128 * i, 128), :], doms[1, pl.ds(128 * i, 128), :] = split(acc)

    @pl.loop(16, 20)
    def _(s):
        service(s)

    core_out[...] = mm3(
        split(rf_out[...].reshape(64, 1024)), got(doms), NN
    ).reshape(8, 8, 128)

    gather_sent(d_hbm, dfull, 0, 512)
    gather_sent(dinv, dinv, 8, 64)

    @pl.loop(0, UNITS)
    def _(u):
        sent(0, u)
        sent(1, u)


def on_device(
    left_factors, mid_factors, row_factors, col_factors, lists, sketch_right, sketch_left, diag_tile
):
    lt = jnp.swapaxes(left_factors, 2, 3).reshape(8, 256, 1024)
    mt = jnp.swapaxes(mid_factors, 2, 3).reshape(8, 256, 1024)
    rt = jnp.swapaxes(row_factors, 1, 2).reshape(256, 1024)
    ct = jnp.swapaxes(col_factors, 1, 2).reshape(256, 1024)
    hbm = pl.BlockSpec(memory_space=pl.ANY)
    vmem = pl.BlockSpec(memory_space=pltpu.VMEM)
    return pl.pallas_call(
        kernel,
        out_shape=(
            jax.ShapeDtypeStruct((8, 64, 128), F32),
            jax.ShapeDtypeStruct((8, 8, 1024), F32),
            jax.ShapeDtypeStruct((8, 8, 128), F32),
        ),
        in_specs=[hbm, hbm, hbm, hbm, vmem, hbm, hbm, hbm],
        out_specs=(vmem, vmem, vmem),
        scratch_shapes=[
            pltpu.VMEM((8, 256, 1024), F32),
            pltpu.VMEM((8, 256, 1024), F32),
            pltpu.VMEM((256, 1024), F32),
            pltpu.VMEM((256, 1024), F32),
            pltpu.VMEM((1024, 128), F32),
            pltpu.VMEM((1024, 128), F32),
            pltpu.VMEM((8, 1024, 128), F32),
            pltpu.VMEM((8, 128, 128), F32),
            pltpu.VMEM((UNITS, 16, 64, 128), F32),
            pltpu.VMEM((UNITS, 8, 32, 128), F32),
            pltpu.VMEM((UNITS, 2, 2, 64, 128), F32),
            pltpu.VMEM((UNITS, 2, 2, 2, 64, 128), F32),
            pltpu.VMEM((UNITS, 2, 1, 32, 128), F32),
            pltpu.VMEM((UNITS, 2, 2, 1, 32, 128), F32),
            pltpu.VMEM((2, 256, 1024), BF16),
            pltpu.VMEM((2, 128, 1024), BF16),
            pltpu.VMEM((2, 128, 256), BF16),
            pltpu.VMEM((2, 256, 1024), BF16),
            pltpu.VMEM((2, 256, 1024), BF16),
            pltpu.VMEM((2, 256, 256), BF16),
            pltpu.VMEM((8, 2, 128, 256), BF16),
            pltpu.VMEM((2, 256, 1024), BF16),
            pltpu.VMEM((2, 1024, 128), BF16),
            pltpu.SemaphoreType.DMA((24,)),
            pltpu.SemaphoreType.DMA((2, UNITS, 6)),
            pltpu.SemaphoreType.DMA((2, UNITS, 6)),
            pltpu.SemaphoreType.DMA((16,)),
            pltpu.SemaphoreType.DMA((16,)),
        ],
        compiler_params=pltpu.CompilerParams(
            collective_id=0, has_side_effects=True, vmem_limit_bytes=58 * 1024 * 1024
        ),
        cost_estimate=pl.CostEstimate(
            flops=6_000_000_000, bytes_accessed=21_000_000, transcendentals=0
        ),
    )(lt, mt, rt, ct, lists, sketch_right, sketch_left, diag_tile)


def solution(mesh):
    placed = (
        P("target", "inner", None, None),
        P("target", "inner", None, None),
        P("inner", None, None),
        P("inner", None, None),
        P("target", None),
        P(),
        P(),
        P(None, "target"),
    )
    return jax.shard_map(
        on_device,
        mesh=mesh,
        in_specs=placed,
        out_specs=(
            P("target", "inner", None),
            P("target", "inner", None),
            P("target", "inner", None),
        ),
        check_vma=False,
    )
```

```python
import functools

import jax
import jax.numpy as jnp
from jax import lax
from jax.experimental import pallas as pl
from jax.experimental.pallas import tpu as pltpu
from jax.sharding import PartitionSpec as P

F32 = jnp.float32
BF16 = jnp.bfloat16
MESH = pl.DeviceIdType.MESH
NN = ((1,), (0,))
NT = ((1,), (1,))
SIDE = 4
UNITS = 16
LAGS = (3, 6, 9, 12)


def split(value):
    high = value.astype(BF16)
    return high, (value - high.astype(F32)).astype(BF16)


def mm(a, b, dims):
    return lax.dot_general(a, b, (dims, ((), ())), preferred_element_type=F32)


def mm3(a, b, dims):
    return mm(a[0], b[0], dims) + (mm(a[1], b[0], dims) + mm(a[0], b[1], dims))


def mm_top(a, b):
    return lax.dot_general(
        a, b, (NN, ((), ())), precision=lax.Precision.HIGHEST, preferred_element_type=F32
    )


def kernel(
    lt_hbm, mt_hbm, rt_hbm, ct_hbm, lists, om_hbm, psi_hbm, d_hbm,
    left_out, rf_out, core_out,
    lt, mt, rt, ct, om, psi, dfull, dinv, part, half, far1, near1, far2, near2,
    rts, psts, cols, ms, ls, cs, ws, rsf,
    in_sem, send_sem, recv_sem, gs_sem, gr_sem,
):
    inner = lax.axis_index("inner")
    target = lax.axis_index("target")
    z, y = inner // SIDE, lax.rem(inner, SIDE)
    x, core = target // 2, lax.rem(target, 2)

    def turn(v, step):
        return lax.rem(v + step, SIDE)

    z_next = (turn(z, 1) * SIDE + y, turn(z, 3) * SIDE + y)
    y_next = (z * SIDE + turn(y, 1), z * SIDE + turn(y, 3))
    x_next = (turn(x, 1) * 2 + core, turn(x, 3) * 2 + core)
    sibling = x * 2 + (1 - core)

    barrier = pltpu.get_barrier_semaphore()
    for peer in z_next + y_next:
        pl.semaphore_signal(barrier, inc=1, device_id=(peer, target), device_id_type=MESH)
    for peer in x_next + (sibling,):
        pl.semaphore_signal(barrier, inc=1, device_id=(inner, peer), device_id_type=MESH)

    loads = []

    def mt_copy(t):
        return pltpu.make_async_copy(mt_hbm.at[t], mt.at[t], in_sem.at[8 + t])

    def lt_copy(t):
        return pltpu.make_async_copy(lt_hbm.at[t], lt.at[t], in_sem.at[16 + t])

    def load(src, dst):
        copy = pltpu.make_async_copy(src, dst, in_sem.at[len(loads)])
        copy.start()
        loads.append(copy)
        return copy

    rt_load = load(rt_hbm, rt)
    mt_copy(0).start()
    ct_load = load(ct_hbm, ct)
    om_load = load(om_hbm, om)
    lt_copy(0).start()
    psi_load = load(psi_hbm, psi)
    d_load = load(d_hbm, dfull.at[target])

    @pl.loop(1, 8)
    def _(t):
        mt_copy(t).start()
        lt_copy(t).start()

    def g_copy(src, dst, sem, peer):
        return pltpu.make_async_remote_copy(
            src_ref=src, dst_ref=dst, send_sem=gs_sem.at[sem], recv_sem=gr_sem.at[sem],
            device_id=(inner, peer), device_id_type=MESH,
        )

    def x_at(step, which):
        return turn(x, step) * 2 + which

    def gather_first(src, dst, base):
        for sem, peer in ((0, x_next[0]), (1, x_next[1]), (4, sibling)):
            g_copy(src, dst.at[target], base + sem, peer).start()

    def gather_second(dst, base, rows):
        before, after = dst.at[x_at(3, core)], dst.at[x_at(1, core)]
        g_copy(before, before, base + 0, sibling).wait_recv()
        g_copy(after, after, base + 1, sibling).wait_recv()
        low, top = before.at[pl.ds(0, rows)], after.at[pl.ds(rows, rows)]
        g_copy(low, low, base + 2, x_next[0]).start()
        g_copy(top, top, base + 3, x_next[1]).start()
        g_copy(before, before, base + 5, sibling).start()
        g_copy(after, after, base + 6, sibling).start()

    def gather_third(dst, base, rows):
        away = dst.at[x_at(2, core)]
        low, top = away.at[pl.ds(0, rows)], away.at[pl.ds(rows, rows)]
        g_copy(low, low, base + 2, sibling).wait_recv()
        g_copy(top, top, base + 3, sibling).wait_recv()
        g_copy(away, away, base + 7, sibling).start()

    def gather_last(dst, base):
        for sem, step in ((4, 0), (5, 3), (6, 1), (7, 2)):
            block = dst.at[x_at(step, 1 - core)]
            g_copy(block, block, base + sem, sibling).wait_recv()

    def gather_sent(src, dst, base, rows):
        for sem in (0, 1, 4, 5, 6, 7):
            g_copy(dst.at[0], dst.at[0], base + sem, sibling).wait_send()
        for sem in (2, 3):
            piece = dst.at[0, pl.ds(0, rows)]
            g_copy(piece, piece, base + sem, sibling).wait_send()

    def place(u, stage):
        axis = lax.rem(u + stage, 2)
        pos = z + axis * (y - z)
        peers = tuple(a + axis * (b - a) for a, b in zip(z_next, y_next))
        return pos, peers

    bufs = ((part, far1, near1, 2), (half, far2, near2, 1))

    def r_copy(stage, u, sem, src, dst, peer):
        return pltpu.make_async_remote_copy(
            src_ref=src, dst_ref=dst,
            send_sem=send_sem.at[stage, u, sem], recv_sem=recv_sem.at[stage, u, sem],
            device_id=(peer, target), device_id_type=MESH,
        )

    def piece(stage, u, chunk, h):
        buf, _, _, w = bufs[stage]
        return buf.at[u, pl.ds((2 * chunk + h) * w, w)]

    def start(stage, u):
        pos, peers = place(u, stage)
        _, far, near, _ = bufs[stage]
        for d in (0, 1):
            r_copy(stage, u, d, piece(stage, u, turn(pos, 2), d), far.at[u, d], peers[d]).start()
        for d in (0, 1):
            r_copy(
                stage, u, 2 + d, piece(stage, u, turn(pos, 1 + 2 * d), 1 - d),
                near.at[u, d, 1 - d], peers[d],
            ).start()

    def middle(stage, u):
        pos, peers = place(u, stage)
        _, far, near, _ = bufs[stage]
        for d in (0, 1):
            own = piece(stage, u, turn(pos, 1 + 2 * d), d)
            r_copy(stage, u, d, far.at[u, d], far.at[u, d], peers[d]).wait_recv()
            own[...] += far[u, d]
            r_copy(stage, u, 4 + d, own, near.at[u, d, d], peers[d]).start()

    def finish(stage, u):
        pos, peers = place(u, stage)
        _, far, near, _ = bufs[stage]
        for d in (0, 1):
            for h in (0, 1):
                sem = 4 + d if h == d else 2 + d
                r_copy(stage, u, sem, near.at[u, d, h], near.at[u, d, h], peers[d]).wait_recv()
        return [
            piece(stage, u, pos, h)[...] + near[u, 0, h] + near[u, 1, h] for h in (0, 1)
        ]

    def sent(stage, u):
        _, far, _, _ = bufs[stage]
        for sem in range(6):
            r_copy(stage, u, sem, far.at[u, 0], far.at[u, 0], z_next[0]).wait_send()

    def finish_first(u):
        for h, value in enumerate(finish(0, u)):
            half[u, pl.ds(4 * h, 4)] = value.reshape(4, 32, 128)
        start(1, u)

    def finish_second(u):
        values = [v.reshape(32, 128) for v in finish(1, u)]

        @pl.when(u >= 8)
        def _():
            for h in (0, 1):
                left_out[u - 8, pl.ds(32 * h, 32), :] = values[h]

        @pl.when(u < 8)
        def _():
            for h in (0, 1):
                for m in range(4):
                    rsf[u, :, pl.ds((4 * h + m) * 128, 128)] = values[h][8 * m : 8 * m + 8]

    def within(s):
        return jnp.logical_and(s >= 0, s < UNITS)

    def service(s):
        a, b, c, d = LAGS
        pl.when(within(s - a))(lambda: middle(0, s - a))
        pl.when(within(s - b))(lambda: finish_first(s - b))
        pl.when(within(s - c))(lambda: middle(1, s - c))
        pl.when(within(s - d))(lambda: finish_second(s - d))

    def chunk_at(u, zz, yy):
        axis = lax.rem(u, 2)
        first, second = zz + axis * (yy - zz), yy + axis * (zz - yy)
        return first * SIDE + second

    def put(ref, value):
        ref[0], ref[1] = split(value)

    def got(ref):
        return ref[0], ref[1]

    rt_load.wait()
    for p in (0, 1):
        pair = split(rt[pl.ds(128 * p, 128), :].T)
        rts[p, :, pl.ds(0, 128)], rts[p, :, pl.ds(128, 128)] = pair
    ct_load.wait()
    om_load.wait()
    put(ws, ct[...])
    put(cols, mm3(got(ws), split(om[...]), NN).T)

    row_tile = lax.broadcasted_iota(jnp.int32, (128, 128), 0) // 64
    col_tile = lax.broadcasted_iota(jnp.int32, (128, 128), 1) // 64
    tile_ids = inner * 4 + lax.broadcasted_iota(jnp.int32, (128, 1), 0) // 64
    cs[...] = jnp.zeros_like(cs)

    def right_unit(t):
        mt_copy(t).wait()
        put(ms, mt[t])
        for p in (0, 1):
            cut = pl.ds(128 * p, 128)
            both = mm(ms[0, cut, :], rts[p], NN)
            coupling = both[:, :128] + (
                both[:, 128:] + mm(ms[1, cut, :], rts[p, :, pl.ds(0, 128)], NN)
            )
            present = jnp.sum(
                (lists[pl.ds(t, 1), :] == tile_ids + 2 * p).astype(F32), axis=1, keepdims=True
            )
            coupling = jnp.where(row_tile == col_tile, coupling, 0.0) * present
            cs[t, 0, cut, cut], cs[t, 1, cut, cut] = split(coupling)
        lt_copy(t).wait()
        put(ls, lt[t])
        both = mm(ls[0], psts[...], NN)
        projected = both[:, :128] + (both[:, 128:] + mm(ls[1], psts[:, pl.ds(0, 128)], NN))
        joined = split(mm3(split(projected.T), got(cs.at[t]), NN))
        for n in range(4):
            cut = pl.ds(256 * n, 256)
            block = mm3(joined, (ws[0, :, cut], ws[1, :, cut]), NN)
            for m in (0, 1):
                value = block[:, 128 * m : 128 * m + 128].reshape(16, 8, 128)
                for i in range(16):
                    part[t, chunk_at(t, i // 4, i % 4), pl.ds((2 * n + m) * 8, 8), :] = value[i]

    def left_unit(t):
        u = t + 8
        inner_left = split(mm3(got(cols), got(cs.at[t]), NT))
        put(ls, lt[t])
        for zz in range(4):
            cut = pl.ds(256 * zz, 256)
            block = mm3(inner_left, (ls[0, :, cut], ls[1, :, cut]), NN).T
            for yy in range(4):
                part[u, chunk_at(u, zz, yy)] = block[64 * yy : 64 * yy + 64]

    def own_inverse():
        d_load.wait()
        block = dfull[target, pl.ds(pl.multiple_of(target * 128, 128), 128), :]
        rows = lax.broadcasted_iota(jnp.int32, (128, 128), 0)
        lanes = lax.broadcasted_iota(jnp.int32, (128, 128), 1)
        eye = (rows == lanes).astype(F32)
        diagonal = jnp.where(rows == lanes, block, 0.0)
        power = eye - block / jnp.sum(diagonal, axis=1, keepdims=True)
        product = eye + power
        for _ in range(6):
            power = mm_top(power, power)
            product = product + mm_top(product, power)
        dinv[target] = product / jnp.sum(diagonal, axis=0, keepdims=True)

    def solve_step(j):
        cut = pl.ds(128 * j, 128)
        rhs = rsf[:, :, cut].reshape(64, 128)
        if j > 0:
            before = pl.ds(0, 128 * j)
            earlier = rf_out[:, :, before].reshape(64, 128 * j)
            rhs = rhs - mm3(split(earlier), split(dfull[j, before, :]), NN)
        rf_out[:, :, cut] = mm3(split(rhs), split(dinv[j]), NN).reshape(8, 8, 128)

    psi_load.wait()
    psts[:, pl.ds(0, 128)], psts[:, pl.ds(128, 128)] = split(psi[...])
    right_unit(0)
    pl.semaphore_wait(barrier, 7)
    start(0, 0)
    gather_first(d_hbm, dfull, 0)

    @pl.loop(1, 8)
    def _(s):
        right_unit(s)
        start(0, s)
        service(s)

    @pl.loop(8, 16)
    def _(s):
        left_unit(s - 8)
        start(0, s)

        @pl.when(s == 12)
        def _():
            gather_second(dfull, 0, 512)

        service(s)

    own_inverse()
    gather_first(dinv.at[target], dinv, 8)
    gather_third(dfull, 0, 512)
    solve_from = max(16, 8 + LAGS[3])

    @pl.loop(16, solve_from)
    def _(s):
        service(s)

        @pl.when(s == 17)
        def _():
            gather_second(dinv, 8, 64)

        @pl.when(s == 18)
        def _():
            gather_third(dinv, 8, 64)

    gather_last(dfull, 0)
    gather_last(dinv, 8)
    for j in range(8):
        solve_step(j)
        if j % 2:
            service(solve_from + j // 2)
    core_out[...] = mm3(
        split(rsf[...].reshape(64, 1024)), split(om[...]), NN
    ).reshape(8, 8, 128)

    @pl.loop(solve_from + 4, 16 + LAGS[3])
    def _(s):
        service(s)

    gather_sent(d_hbm, dfull, 0, 512)
    gather_sent(dinv, dinv, 8, 64)

    @pl.loop(0, UNITS)
    def _(u):
        sent(0, u)
        sent(1, u)


def hand_over(a, b, c, a_out, b_out, c_out):
    a_out[...] = a[...]
    b_out[...] = b[...]
    c_out[...] = c[...]


def on_device(
    left_factors, mid_factors, row_factors, col_factors, lists, sketch_right, sketch_left, diag_tile
):
    lt = jnp.swapaxes(left_factors, 2, 3).reshape(8, 256, 1024)
    mt = jnp.swapaxes(mid_factors, 2, 3).reshape(8, 256, 1024)
    rt = jnp.swapaxes(row_factors, 1, 2).reshape(256, 1024)
    ct = jnp.swapaxes(col_factors, 1, 2).reshape(256, 1024)
    hbm = pl.BlockSpec(memory_space=pl.ANY)
    vmem = pl.BlockSpec(memory_space=pltpu.VMEM)
    parts = pl.pallas_call(
        kernel,
        out_shape=(
            jax.ShapeDtypeStruct((8, 64, 128), F32),
            jax.ShapeDtypeStruct((8, 8, 1024), F32),
            jax.ShapeDtypeStruct((8, 8, 128), F32),
        ),
        in_specs=[hbm, hbm, hbm, hbm, vmem, hbm, hbm, hbm],
        out_specs=(vmem, vmem, vmem),
        scratch_shapes=[
            pltpu.VMEM((8, 256, 1024), F32),
            pltpu.VMEM((8, 256, 1024), F32),
            pltpu.VMEM((256, 1024), F32),
            pltpu.VMEM((256, 1024), F32),
            pltpu.VMEM((1024, 128), F32),
            pltpu.VMEM((1024, 128), F32),
            pltpu.VMEM((8, 1024, 128), F32),
            pltpu.VMEM((8, 128, 128), F32),
            pltpu.VMEM((UNITS, 16, 64, 128), F32),
            pltpu.VMEM((UNITS, 8, 32, 128), F32),
            pltpu.VMEM((UNITS, 2, 2, 64, 128), F32),
            pltpu.VMEM((UNITS, 2, 2, 2, 64, 128), F32),
            pltpu.VMEM((UNITS, 2, 1, 32, 128), F32),
            pltpu.VMEM((UNITS, 2, 2, 1, 32, 128), F32),
            pltpu.VMEM((2, 1024, 256), BF16),
            pltpu.VMEM((1024, 256), BF16),
            pltpu.VMEM((2, 128, 256), BF16),
            pltpu.VMEM((2, 256, 1024), BF16),
            pltpu.VMEM((2, 256, 1024), BF16),
            pltpu.VMEM((8, 2, 256, 256), BF16),
            pltpu.VMEM((2, 256, 1024), BF16),
            pltpu.VMEM((8, 8, 1024), F32),
            pltpu.SemaphoreType.DMA((24,)),
            pltpu.SemaphoreType.DMA((2, UNITS, 6)),
            pltpu.SemaphoreType.DMA((2, UNITS, 6)),
            pltpu.SemaphoreType.DMA((16,)),
            pltpu.SemaphoreType.DMA((16,)),
        ],
        compiler_params=pltpu.CompilerParams(
            collective_id=0, has_side_effects=True, vmem_limit_bytes=58 * 1024 * 1024
        ),
        cost_estimate=pl.CostEstimate(
            flops=6_000_000_000, bytes_accessed=21_000_000, transcendentals=0
        ),
    )(lt, mt, rt, ct, lists, sketch_right, sketch_left, diag_tile)
    return pl.pallas_call(
        hand_over,
        out_shape=tuple(jax.ShapeDtypeStruct(p.shape, F32) for p in parts),
        in_specs=[vmem] * 3,
        out_specs=(vmem,) * 3,
        cost_estimate=pl.CostEstimate(flops=0, bytes_accessed=1_200_000, transcendentals=0),
    )(*parts)


def solution(mesh):
    placed = (
        P("target", "inner", None, None),
        P("target", "inner", None, None),
        P("inner", None, None),
        P("inner", None, None),
        P("target", None),
        P(),
        P(),
        P(None, "target"),
    )
    return jax.shard_map(
        on_device,
        mesh=mesh,
        in_specs=placed,
        out_specs=(
            P("target", "inner", None),
            P("target", "inner", None),
            P("target", "inner", None),
        ),
        check_vma=False,
    )
```

```python
import functools

import jax
import jax.numpy as jnp
from jax import lax
from jax.experimental import pallas as pl
from jax.experimental.pallas import tpu as pltpu
from jax.sharding import PartitionSpec as P

F32 = jnp.float32
BF16 = jnp.bfloat16
MESH = pl.DeviceIdType.MESH
NN = ((1,), (0,))
NT = ((1,), (1,))
SIDE = 4
UNITS = 16
LAGS = (3, 6, 9, 12)


def split(value):
    high = value.astype(BF16)
    return high, (value - high.astype(F32)).astype(BF16)


def mm(a, b, dims):
    return lax.dot_general(a, b, (dims, ((), ())), preferred_element_type=F32)


def mm3(a, b, dims):
    return mm(a[0], b[0], dims) + (mm(a[1], b[0], dims) + mm(a[0], b[1], dims))


def mm_top(a, b):
    return lax.dot_general(
        a, b, (NN, ((), ())), precision=lax.Precision.HIGHEST, preferred_element_type=F32
    )


def kernel(
    lt_hbm, mt_hbm, rt_hbm, ct_hbm, lists, om_hbm, psi_hbm, d_hbm,
    left_out, rf_out, core_out,
    lt, mt, rt, ct, om, psi, dfull, dinv, part, half, far1, near1, far2, near2,
    rts, psts, cols, ms, ls, cs, ws, rsf,
    in_sem, send_sem, recv_sem, gs_sem, gr_sem,
):
    inner = lax.axis_index("inner")
    target = lax.axis_index("target")
    z, y = inner // SIDE, lax.rem(inner, SIDE)
    x, core = target // 2, lax.rem(target, 2)

    def turn(v, step):
        return lax.rem(v + step, SIDE)

    z_next = (turn(z, 1) * SIDE + y, turn(z, 3) * SIDE + y)
    y_next = (z * SIDE + turn(y, 1), z * SIDE + turn(y, 3))
    x_next = (turn(x, 1) * 2 + core, turn(x, 3) * 2 + core)
    sibling = x * 2 + (1 - core)

    barrier = pltpu.get_barrier_semaphore()
    for peer in z_next + y_next:
        pl.semaphore_signal(barrier, inc=1, device_id=(peer, target), device_id_type=MESH)
    for peer in x_next + (sibling,):
        pl.semaphore_signal(barrier, inc=1, device_id=(inner, peer), device_id_type=MESH)

    loads = []

    def mt_copy(t):
        return pltpu.make_async_copy(mt_hbm.at[t], mt.at[t], in_sem.at[8 + t])

    def lt_copy(t):
        return pltpu.make_async_copy(lt_hbm.at[t], lt.at[t], in_sem.at[16 + t])

    def load(src, dst):
        copy = pltpu.make_async_copy(src, dst, in_sem.at[len(loads)])
        copy.start()
        loads.append(copy)
        return copy

    rt_load = load(rt_hbm, rt)
    mt_copy(0).start()
    ct_load = load(ct_hbm, ct)
    om_load = load(om_hbm, om)
    lt_copy(0).start()
    psi_load = load(psi_hbm, psi)
    d_load = load(d_hbm, dfull.at[target])

    @pl.loop(1, 8)
    def _(t):
        mt_copy(t).start()
        lt_copy(t).start()

    def g_copy(src, dst, sem, peer):
        return pltpu.make_async_remote_copy(
            src_ref=src, dst_ref=dst, send_sem=gs_sem.at[sem], recv_sem=gr_sem.at[sem],
            device_id=(inner, peer), device_id_type=MESH,
        )

    def x_at(step, which):
        return turn(x, step) * 2 + which

    def gather_first(src, dst, base):
        for sem, peer in ((0, x_next[0]), (1, x_next[1]), (4, sibling)):
            g_copy(src, dst.at[target], base + sem, peer).start()

    def gather_second(dst, base, rows):
        before, after = dst.at[x_at(3, core)], dst.at[x_at(1, core)]
        g_copy(before, before, base + 0, sibling).wait_recv()
        g_copy(after, after, base + 1, sibling).wait_recv()
        low, top = before.at[pl.ds(0, rows)], after.at[pl.ds(rows, rows)]
        g_copy(low, low, base + 2, x_next[0]).start()
        g_copy(top, top, base + 3, x_next[1]).start()
        g_copy(before, before, base + 5, sibling).start()
        g_copy(after, after, base + 6, sibling).start()

    def gather_third(dst, base, rows):
        away = dst.at[x_at(2, core)]
        low, top = away.at[pl.ds(0, rows)], away.at[pl.ds(rows, rows)]
        g_copy(low, low, base + 2, sibling).wait_recv()
        g_copy(top, top, base + 3, sibling).wait_recv()
        g_copy(away, away, base + 7, sibling).start()

    def gather_last(dst, base):
        for sem, step in ((4, 0), (5, 3), (6, 1), (7, 2)):
            block = dst.at[x_at(step, 1 - core)]
            g_copy(block, block, base + sem, sibling).wait_recv()

    def gather_sent(src, dst, base, rows):
        for sem in (0, 1, 4, 5, 6, 7):
            g_copy(dst.at[0], dst.at[0], base + sem, sibling).wait_send()
        for sem in (2, 3):
            piece = dst.at[0, pl.ds(0, rows)]
            g_copy(piece, piece, base + sem, sibling).wait_send()

    def place(u, stage):
        axis = lax.rem(u + stage, 2)
        pos = z + axis * (y - z)
        peers = tuple(a + axis * (b - a) for a, b in zip(z_next, y_next))
        return pos, peers

    bufs = ((part, far1, near1, 2), (half, far2, near2, 1))

    def r_copy(stage, u, sem, src, dst, peer):
        return pltpu.make_async_remote_copy(
            src_ref=src, dst_ref=dst,
            send_sem=send_sem.at[stage, min(sem // 2, 1)], recv_sem=recv_sem.at[stage, u, sem],
            device_id=(peer, target), device_id_type=MESH,
        )

    def piece(stage, u, chunk, h):
        buf, _, _, w = bufs[stage]
        return buf.at[u, pl.ds((2 * chunk + h) * w, w)]

    def start(stage, u):
        pos, peers = place(u, stage)
        _, far, near, _ = bufs[stage]
        for d in (0, 1):
            r_copy(stage, u, d, piece(stage, u, turn(pos, 2), d), far.at[u, d], peers[d]).start()
        for d in (0, 1):
            r_copy(
                stage, u, 2 + d, piece(stage, u, turn(pos, 1 + 2 * d), 1 - d),
                near.at[u, d, 1 - d], peers[d],
            ).start()

    def middle(stage, u):
        pos, peers = place(u, stage)
        _, far, near, _ = bufs[stage]
        for d in (0, 1):
            own = piece(stage, u, turn(pos, 1 + 2 * d), d)
            r_copy(stage, u, d, far.at[u, d], far.at[u, d], peers[d]).wait_recv()
            own[...] += far[u, d]
            r_copy(stage, u, 4 + d, own, near.at[u, d, d], peers[d]).start()

    def finish(stage, u):
        pos, peers = place(u, stage)
        _, far, near, _ = bufs[stage]
        for d in (0, 1):
            for h in (0, 1):
                sem = 4 + d if h == d else 2 + d
                r_copy(stage, u, sem, near.at[u, d, h], near.at[u, d, h], peers[d]).wait_recv()
        return [
            piece(stage, u, pos, h)[...] + near[u, 0, h] + near[u, 1, h] for h in (0, 1)
        ]

    def sent(stage):
        _, far, near, _ = bufs[stage]
        r_copy(stage, 0, 0, far, far, z_next[0]).wait_send()
        r_copy(stage, 0, 2, near, near, z_next[0]).wait_send()

    def finish_first(u):
        for h, value in enumerate(finish(0, u)):
            half[u, pl.ds(4 * h, 4)] = value.reshape(4, 32, 128)
        start(1, u)

    def finish_second(u):
        values = [v.reshape(32, 128) for v in finish(1, u)]

        @pl.when(u >= 8)
        def _():
            for h in (0, 1):
                left_out[u - 8, pl.ds(32 * h, 32), :] = values[h]

        @pl.when(u < 8)
        def _():
            for h in (0, 1):
                for m in range(4):
                    rsf[u, :, pl.ds((4 * h + m) * 128, 128)] = values[h][8 * m : 8 * m + 8]

    def within(s):
        return jnp.logical_and(s >= 0, s < UNITS)

    def service(s):
        a, b, c, d = LAGS
        pl.when(within(s - a))(lambda: middle(0, s - a))
        pl.when(within(s - b))(lambda: finish_first(s - b))
        pl.when(within(s - c))(lambda: middle(1, s - c))
        pl.when(within(s - d))(lambda: finish_second(s - d))

    def chunk_at(u, zz, yy):
        axis = lax.rem(u, 2)
        first, second = zz + axis * (yy - zz), yy + axis * (zz - yy)
        return first * SIDE + second

    def put(ref, value):
        ref[0], ref[1] = split(value)

    def got(ref):
        return ref[0], ref[1]

    rt_load.wait()
    for p in (0, 1):
        pair = split(rt[pl.ds(128 * p, 128), :].T)
        rts[p, :, pl.ds(0, 128)], rts[p, :, pl.ds(128, 128)] = pair
    ct_load.wait()
    om_load.wait()
    put(ws, ct[...])
    put(cols, mm3(got(ws), split(om[...]), NN).T)

    row_tile = lax.broadcasted_iota(jnp.int32, (128, 128), 0) // 64
    col_tile = lax.broadcasted_iota(jnp.int32, (128, 128), 1) // 64
    tile_ids = inner * 4 + lax.broadcasted_iota(jnp.int32, (128, 1), 0) // 64
    cs[...] = jnp.zeros_like(cs)

    def right_unit(t):
        mt_copy(t).wait()
        put(ms, mt[t])
        for p in (0, 1):
            cut = pl.ds(128 * p, 128)
            both = mm(ms[0, cut, :], rts[p], NN)
            coupling = both[:, :128] + (
                both[:, 128:] + mm(ms[1, cut, :], rts[p, :, pl.ds(0, 128)], NN)
            )
            present = jnp.sum(
                (lists[pl.ds(t, 1), :] == tile_ids + 2 * p).astype(F32), axis=1, keepdims=True
            )
            coupling = jnp.where(row_tile == col_tile, coupling, 0.0) * present
            cs[t, 0, cut, cut], cs[t, 1, cut, cut] = split(coupling)
        lt_copy(t).wait()
        put(ls, lt[t])
        both = mm(ls[0], psts[...], NN)
        projected = both[:, :128] + (both[:, 128:] + mm(ls[1], psts[:, pl.ds(0, 128)], NN))
        joined = split(mm3(split(projected.T), got(cs.at[t]), NN))
        for n in range(4):
            cut = pl.ds(256 * n, 256)
            block = mm3(joined, (ws[0, :, cut], ws[1, :, cut]), NN)
            for m in (0, 1):
                value = block[:, 128 * m : 128 * m + 128].reshape(16, 8, 128)
                for i in range(16):
                    part[t, chunk_at(t, i // 4, i % 4), pl.ds((2 * n + m) * 8, 8), :] = value[i]

    def left_unit(t):
        u = t + 8
        inner_left = split(mm3(got(cols), got(cs.at[t]), NT))
        put(ls, lt[t])
        for zz in range(4):
            cut = pl.ds(256 * zz, 256)
            block = mm3(inner_left, (ls[0, :, cut], ls[1, :, cut]), NN).T
            for yy in range(4):
                part[u, chunk_at(u, zz, yy)] = block[64 * yy : 64 * yy + 64]

    def own_inverse():
        d_load.wait()
        block = dfull[target, pl.ds(pl.multiple_of(target * 128, 128), 128), :]
        rows = lax.broadcasted_iota(jnp.int32, (128, 128), 0)
        lanes = lax.broadcasted_iota(jnp.int32, (128, 128), 1)
        eye = (rows == lanes).astype(F32)
        diagonal = jnp.where(rows == lanes, block, 0.0)
        power = eye - block / jnp.sum(diagonal, axis=1, keepdims=True)
        product = eye + power
        for _ in range(6):
            power = mm_top(power, power)
            product = product + mm_top(product, power)
        dinv[target] = product / jnp.sum(diagonal, axis=0, keepdims=True)

    def solve_step(j):
        cut = pl.ds(128 * j, 128)
        rhs = rsf[:, :, cut].reshape(64, 128)
        if j > 0:
            before = pl.ds(0, 128 * j)
            earlier = rf_out[:, :, before].reshape(64, 128 * j)
            rhs = rhs - mm3(split(earlier), split(dfull[j, before, :]), NN)
        rf_out[:, :, cut] = mm3(split(rhs), split(dinv[j]), NN).reshape(8, 8, 128)

    psi_load.wait()
    psts[:, pl.ds(0, 128)], psts[:, pl.ds(128, 128)] = split(psi[...])
    right_unit(0)
    pl.semaphore_wait(barrier, 7)
    start(0, 0)
    gather_first(d_hbm, dfull, 0)

    @pl.loop(1, 8)
    def _(s):
        right_unit(s)
        start(0, s)
        service(s)

    @pl.loop(8, 16)
    def _(s):
        left_unit(s - 8)
        start(0, s)

        @pl.when(s == 9)
        def _():
            own_inverse()
            gather_first(dinv.at[target], dinv, 8)

        @pl.when(s == 12)
        def _():
            gather_second(dfull, 0, 512)
            gather_second(dinv, 8, 64)

        @pl.when(s == 15)
        def _():
            gather_third(dfull, 0, 512)
            gather_third(dinv, 8, 64)

        service(s)

    solve_from = max(16, 8 + LAGS[3])

    @pl.loop(16, solve_from)
    def _(s):
        service(s)

    gather_last(dfull, 0)
    gather_last(dinv, 8)
    for j in range(8):
        solve_step(j)
        if j % 2:
            service(solve_from + j // 2)
    core_out[...] = mm3(
        split(rsf[...].reshape(64, 1024)), split(om[...]), NN
    ).reshape(8, 8, 128)

    @pl.loop(solve_from + 4, 16 + LAGS[3])
    def _(s):
        service(s)

    gather_sent(d_hbm, dfull, 0, 512)
    gather_sent(dinv, dinv, 8, 64)

    sent(0)
    sent(1)


def hand_over(a, b, c, a_out, b_out, c_out):
    a_out[...] = a[...]
    b_out[...] = b[...]
    c_out[...] = c[...]


def on_device(
    left_factors, mid_factors, row_factors, col_factors, lists, sketch_right, sketch_left, diag_tile
):
    lt = jnp.swapaxes(left_factors, 2, 3).reshape(8, 256, 1024)
    mt = jnp.swapaxes(mid_factors, 2, 3).reshape(8, 256, 1024)
    rt = jnp.swapaxes(row_factors, 1, 2).reshape(256, 1024)
    ct = jnp.swapaxes(col_factors, 1, 2).reshape(256, 1024)
    hbm = pl.BlockSpec(memory_space=pl.ANY)
    vmem = pl.BlockSpec(memory_space=pltpu.VMEM)
    parts = pl.pallas_call(
        kernel,
        out_shape=(
            jax.ShapeDtypeStruct((8, 64, 128), F32),
            jax.ShapeDtypeStruct((8, 8, 1024), F32),
            jax.ShapeDtypeStruct((8, 8, 128), F32),
        ),
        in_specs=[hbm, hbm, hbm, hbm, vmem, hbm, hbm, hbm],
        out_specs=(vmem, vmem, vmem),
        scratch_shapes=[
            pltpu.VMEM((8, 256, 1024), F32),
            pltpu.VMEM((8, 256, 1024), F32),
            pltpu.VMEM((256, 1024), F32),
            pltpu.VMEM((256, 1024), F32),
            pltpu.VMEM((1024, 128), F32),
            pltpu.VMEM((1024, 128), F32),
            pltpu.VMEM((8, 1024, 128), F32),
            pltpu.VMEM((8, 128, 128), F32),
            pltpu.VMEM((UNITS, 16, 64, 128), F32),
            pltpu.VMEM((UNITS, 8, 32, 128), F32),
            pltpu.VMEM((UNITS, 2, 2, 64, 128), F32),
            pltpu.VMEM((UNITS, 2, 2, 2, 64, 128), F32),
            pltpu.VMEM((UNITS, 2, 1, 32, 128), F32),
            pltpu.VMEM((UNITS, 2, 2, 1, 32, 128), F32),
            pltpu.VMEM((2, 1024, 256), BF16),
            pltpu.VMEM((1024, 256), BF16),
            pltpu.VMEM((2, 128, 256), BF16),
            pltpu.VMEM((2, 256, 1024), BF16),
            pltpu.VMEM((2, 256, 1024), BF16),
            pltpu.VMEM((8, 2, 256, 256), BF16),
            pltpu.VMEM((2, 256, 1024), BF16),
            pltpu.VMEM((8, 8, 1024), F32),
            pltpu.SemaphoreType.DMA((24,)),
            pltpu.SemaphoreType.DMA((2, 2)),
            pltpu.SemaphoreType.DMA((2, UNITS, 6)),
            pltpu.SemaphoreType.DMA((16,)),
            pltpu.SemaphoreType.DMA((16,)),
        ],
        compiler_params=pltpu.CompilerParams(
            collective_id=0, has_side_effects=True, vmem_limit_bytes=58 * 1024 * 1024
        ),
        cost_estimate=pl.CostEstimate(
            flops=6_000_000_000, bytes_accessed=21_000_000, transcendentals=0
        ),
    )(lt, mt, rt, ct, lists, sketch_right, sketch_left, diag_tile)
    return pl.pallas_call(
        hand_over,
        out_shape=tuple(jax.ShapeDtypeStruct(p.shape, F32) for p in parts),
        in_specs=[vmem] * 3,
        out_specs=(vmem,) * 3,
        cost_estimate=pl.CostEstimate(flops=0, bytes_accessed=1_200_000, transcendentals=0),
    )(*parts)


def solution(mesh):
    placed = (
        P("target", "inner", None, None),
        P("target", "inner", None, None),
        P("inner", None, None),
        P("inner", None, None),
        P("target", None),
        P(),
        P(),
        P(None, "target"),
    )
    return jax.shard_map(
        on_device,
        mesh=mesh,
        in_specs=placed,
        out_specs=(
            P("target", "inner", None),
            P("target", "inner", None),
            P("target", "inner", None),
        ),
        check_vma=False,
    )
```

```python
import functools

import jax
import jax.numpy as jnp
from jax import lax
from jax.experimental import pallas as pl
from jax.experimental.pallas import tpu as pltpu
from jax.sharding import PartitionSpec as P

F32 = jnp.float32
BF16 = jnp.bfloat16
MESH = pl.DeviceIdType.MESH
NN = ((1,), (0,))
NT = ((1,), (1,))
SIDE = 4
UNITS = 16
LAGS = (3, 6, 9, 12)


def split(value):
    high = value.astype(BF16)
    return high, (value - high.astype(F32)).astype(BF16)


def mm(a, b, dims):
    return lax.dot_general(a, b, (dims, ((), ())), preferred_element_type=F32)


def mm3(a, b, dims):
    return mm(a[0], b[0], dims) + (mm(a[1], b[0], dims) + mm(a[0], b[1], dims))


def mm_top(a, b):
    return lax.dot_general(
        a, b, (NN, ((), ())), precision=lax.Precision.HIGHEST, preferred_element_type=F32
    )


def kernel(
    lt_hbm, mt_hbm, rt_hbm, ct_hbm, lists, om_hbm, psi_hbm, d_hbm,
    left_out, rf_out, core_out,
    lt, mt, rt, ct, om, psi, dfull, dinv, part, half, far1, near1, far2, near2,
    rts, psts, cols, ms, ls, cs, ws, rsf,
    in_sem, send_sem, recv_sem, gs_sem, gr_sem,
):
    inner = lax.axis_index("inner")
    target = lax.axis_index("target")
    z, y = inner // SIDE, lax.rem(inner, SIDE)
    x, core = target // 2, lax.rem(target, 2)

    def turn(v, step):
        return lax.rem(v + step, SIDE)

    z_next = (turn(z, 1) * SIDE + y, turn(z, 3) * SIDE + y)
    y_next = (z * SIDE + turn(y, 1), z * SIDE + turn(y, 3))
    x_next = (turn(x, 1) * 2 + core, turn(x, 3) * 2 + core)
    sibling = x * 2 + (1 - core)

    barrier = pltpu.get_barrier_semaphore()
    for peer in z_next + y_next:
        pl.semaphore_signal(barrier, inc=1, device_id=(peer, target), device_id_type=MESH)
    for peer in x_next + (sibling,):
        pl.semaphore_signal(barrier, inc=1, device_id=(inner, peer), device_id_type=MESH)

    loads = []

    def mt_copy(t):
        return pltpu.make_async_copy(mt_hbm.at[t], mt.at[t], in_sem.at[8 + t])

    def lt_copy(t):
        return pltpu.make_async_copy(lt_hbm.at[t], lt.at[t], in_sem.at[16 + t])

    def load(src, dst):
        copy = pltpu.make_async_copy(src, dst, in_sem.at[len(loads)])
        copy.start()
        loads.append(copy)
        return copy

    rt_load = load(rt_hbm, rt)
    mt_copy(0).start()
    ct_load = load(ct_hbm, ct)
    om_load = load(om_hbm, om)
    lt_copy(0).start()
    psi_load = load(psi_hbm, psi)
    d_load = load(d_hbm, dfull.at[target])

    @pl.loop(1, 8)
    def _(t):
        mt_copy(t).start()
        lt_copy(t).start()

    def g_copy(src, dst, sem, peer):
        return pltpu.make_async_remote_copy(
            src_ref=src, dst_ref=dst, send_sem=gs_sem.at[sem], recv_sem=gr_sem.at[sem],
            device_id=(inner, peer), device_id_type=MESH,
        )

    def x_at(step, which):
        return turn(x, step) * 2 + which

    def gather_first(src, dst, base):
        for sem, peer in ((0, x_next[0]), (1, x_next[1]), (4, sibling)):
            g_copy(src, dst.at[target], base + sem, peer).start()

    def gather_second(dst, base, rows):
        before, after = dst.at[x_at(3, core)], dst.at[x_at(1, core)]
        g_copy(before, before, base + 0, sibling).wait_recv()
        g_copy(after, after, base + 1, sibling).wait_recv()
        low, top = before.at[pl.ds(0, rows)], after.at[pl.ds(rows, rows)]
        g_copy(low, low, base + 2, x_next[0]).start()
        g_copy(top, top, base + 3, x_next[1]).start()
        g_copy(before, before, base + 5, sibling).start()
        g_copy(after, after, base + 6, sibling).start()

    def gather_third(dst, base, rows):
        away = dst.at[x_at(2, core)]
        low, top = away.at[pl.ds(0, rows)], away.at[pl.ds(rows, rows)]
        g_copy(low, low, base + 2, sibling).wait_recv()
        g_copy(top, top, base + 3, sibling).wait_recv()
        g_copy(away, away, base + 7, sibling).start()

    def gather_last(dst, base):
        for sem, step in ((4, 0), (5, 3), (6, 1), (7, 2)):
            block = dst.at[x_at(step, 1 - core)]
            g_copy(block, block, base + sem, sibling).wait_recv()

    def gather_sent(src, dst, base, rows):
        for sem in (0, 1, 4, 5, 6, 7):
            g_copy(dst.at[0], dst.at[0], base + sem, sibling).wait_send()
        for sem in (2, 3):
            piece = dst.at[0, pl.ds(0, rows)]
            g_copy(piece, piece, base + sem, sibling).wait_send()

    def place(u, stage):
        axis = lax.rem(u + stage, 2)
        pos = z + axis * (y - z)
        peers = tuple(a + axis * (b - a) for a, b in zip(z_next, y_next))
        return pos, peers

    bufs = ((part, far1, near1, 2), (half, far2, near2, 1))

    def r_copy(stage, u, sem, src, dst, peer):
        return pltpu.make_async_remote_copy(
            src_ref=src, dst_ref=dst,
            send_sem=send_sem.at[stage, min(sem // 2, 1)], recv_sem=recv_sem.at[stage, u, min(sem // 2, 1)],
            device_id=(peer, target), device_id_type=MESH,
        )

    def piece(stage, u, chunk, h):
        buf, _, _, w = bufs[stage]
        return buf.at[u, pl.ds((2 * chunk + h) * w, w)]

    def start(stage, u):
        pos, peers = place(u, stage)
        _, far, near, _ = bufs[stage]
        for d in (0, 1):
            r_copy(stage, u, d, piece(stage, u, turn(pos, 2), d), far.at[u, d], peers[d]).start()
        for d in (0, 1):
            r_copy(
                stage, u, 2 + d, piece(stage, u, turn(pos, 1 + 2 * d), 1 - d),
                near.at[u, d, 1 - d], peers[d],
            ).start()

    def middle(stage, u):
        pos, peers = place(u, stage)
        _, far, near, _ = bufs[stage]
        r_copy(stage, u, 0, far.at[u], far.at[u], peers[0]).wait_recv()
        for d in (0, 1):
            own = piece(stage, u, turn(pos, 1 + 2 * d), d)
            own[...] += far[u, d]
            r_copy(stage, u, 4 + d, own, near.at[u, d, d], peers[d]).start()

    def finish(stage, u):
        pos, peers = place(u, stage)
        _, far, near, _ = bufs[stage]
        r_copy(stage, u, 2, near.at[u], near.at[u], peers[0]).wait_recv()
        return [
            piece(stage, u, pos, h)[...] + near[u, 0, h] + near[u, 1, h] for h in (0, 1)
        ]

    def sent(stage):
        _, far, near, _ = bufs[stage]
        r_copy(stage, 0, 0, far, far, z_next[0]).wait_send()
        r_copy(stage, 0, 2, near, near, z_next[0]).wait_send()

    def finish_first(u):
        for h, value in enumerate(finish(0, u)):
            half[u, pl.ds(4 * h, 4)] = value.reshape(4, 32, 128)
        start(1, u)

    def finish_second(u):
        values = [v.reshape(32, 128) for v in finish(1, u)]

        @pl.when(u >= 8)
        def _():
            for h in (0, 1):
                left_out[u - 8, pl.ds(32 * h, 32), :] = values[h]

        @pl.when(u < 8)
        def _():
            for h in (0, 1):
                for m in range(4):
                    rsf[u, :, pl.ds((4 * h + m) * 128, 128)] = values[h][8 * m : 8 * m + 8]

    def within(s):
        return jnp.logical_and(s >= 0, s < UNITS)

    def service(s):
        a, b, c, d = LAGS
        pl.when(within(s - a))(lambda: middle(0, s - a))
        pl.when(within(s - b))(lambda: finish_first(s - b))
        pl.when(within(s - c))(lambda: middle(1, s - c))
        pl.when(within(s - d))(lambda: finish_second(s - d))

    def chunk_at(u, zz, yy):
        axis = lax.rem(u, 2)
        first, second = zz + axis * (yy - zz), yy + axis * (zz - yy)
        return first * SIDE + second

    def put(ref, value):
        ref[0], ref[1] = split(value)

    def got(ref):
        return ref[0], ref[1]

    rt_load.wait()
    for p in (0, 1):
        pair = split(rt[pl.ds(128 * p, 128), :].T)
        rts[p, :, pl.ds(0, 128)], rts[p, :, pl.ds(128, 128)] = pair
    ct_load.wait()
    om_load.wait()
    put(ws, ct[...])
    put(cols, mm3(got(ws), split(om[...]), NN).T)

    row_tile = lax.broadcasted_iota(jnp.int32, (128, 128), 0) // 64
    col_tile = lax.broadcasted_iota(jnp.int32, (128, 128), 1) // 64
    tile_ids = inner * 4 + lax.broadcasted_iota(jnp.int32, (128, 1), 0) // 64
    cs[...] = jnp.zeros_like(cs)

    def right_unit(t):
        mt_copy(t).wait()
        put(ms, mt[t])
        for p in (0, 1):
            cut = pl.ds(128 * p, 128)
            both = mm(ms[0, cut, :], rts[p], NN)
            coupling = both[:, :128] + (
                both[:, 128:] + mm(ms[1, cut, :], rts[p, :, pl.ds(0, 128)], NN)
            )
            present = jnp.sum(
                (lists[pl.ds(t, 1), :] == tile_ids + 2 * p).astype(F32), axis=1, keepdims=True
            )
            coupling = jnp.where(row_tile == col_tile, coupling, 0.0) * present
            cs[t, 0, cut, cut], cs[t, 1, cut, cut] = split(coupling)
        lt_copy(t).wait()
        put(ls, lt[t])
        both = mm(ls[0], psts[...], NN)
        projected = both[:, :128] + (both[:, 128:] + mm(ls[1], psts[:, pl.ds(0, 128)], NN))
        joined = split(mm3(split(projected.T), got(cs.at[t]), NN))
        for n in range(4):
            cut = pl.ds(256 * n, 256)
            block = mm3(joined, (ws[0, :, cut], ws[1, :, cut]), NN)
            for m in (0, 1):
                value = block[:, 128 * m : 128 * m + 128].reshape(16, 8, 128)
                for i in range(16):
                    part[t, chunk_at(t, i // 4, i % 4), pl.ds((2 * n + m) * 8, 8), :] = value[i]

    def left_unit(t):
        u = t + 8
        inner_left = split(mm3(got(cols), got(cs.at[t]), NT))
        put(ls, lt[t])
        for zz in range(4):
            cut = pl.ds(256 * zz, 256)
            block = mm3(inner_left, (ls[0, :, cut], ls[1, :, cut]), NN).T
            for yy in range(4):
                part[u, chunk_at(u, zz, yy)] = block[64 * yy : 64 * yy + 64]

    def own_inverse():
        d_load.wait()
        block = dfull[target, pl.ds(pl.multiple_of(target * 128, 128), 128), :]
        rows = lax.broadcasted_iota(jnp.int32, (128, 128), 0)
        lanes = lax.broadcasted_iota(jnp.int32, (128, 128), 1)
        eye = (rows == lanes).astype(F32)
        diagonal = jnp.where(rows == lanes, block, 0.0)
        power = eye - block / jnp.sum(diagonal, axis=1, keepdims=True)
        product = eye + power
        for _ in range(6):
            power = mm_top(power, power)
            product = product + mm_top(product, power)
        dinv[target] = product / jnp.sum(diagonal, axis=0, keepdims=True)

    def solve_step(j):
        cut = pl.ds(128 * j, 128)
        rhs = rsf[:, :, cut].reshape(64, 128)
        if j > 0:
            before = pl.ds(0, 128 * j)
            earlier = rf_out[:, :, before].reshape(64, 128 * j)
            rhs = rhs - mm3(split(earlier), split(dfull[j, before, :]), NN)
        rf_out[:, :, cut] = mm3(split(rhs), split(dinv[j]), NN).reshape(8, 8, 128)

    psi_load.wait()
    psts[:, pl.ds(0, 128)], psts[:, pl.ds(128, 128)] = split(psi[...])
    right_unit(0)
    pl.semaphore_wait(barrier, 7)
    start(0, 0)
    gather_first(d_hbm, dfull, 0)

    @pl.loop(1, 8)
    def _(s):
        right_unit(s)
        start(0, s)
        service(s)

    @pl.loop(8, 16)
    def _(s):
        left_unit(s - 8)
        start(0, s)

        @pl.when(s == 9)
        def _():
            own_inverse()
            gather_first(dinv.at[target], dinv, 8)

        @pl.when(s == 12)
        def _():
            gather_second(dfull, 0, 512)
            gather_second(dinv, 8, 64)

        @pl.when(s == 15)
        def _():
            gather_third(dfull, 0, 512)
            gather_third(dinv, 8, 64)

        service(s)

    solve_from = max(16, 8 + LAGS[3])

    @pl.loop(16, solve_from)
    def _(s):
        service(s)

    gather_last(dfull, 0)
    gather_last(dinv, 8)
    for j in range(8):
        solve_step(j)
        if j % 2:
            service(solve_from + j // 2)
    core_out[...] = mm3(
        split(rsf[...].reshape(64, 1024)), split(om[...]), NN
    ).reshape(8, 8, 128)

    @pl.loop(solve_from + 4, 16 + LAGS[3])
    def _(s):
        service(s)

    gather_sent(d_hbm, dfull, 0, 512)
    gather_sent(dinv, dinv, 8, 64)

    sent(0)
    sent(1)


def hand_over(a, b, c, a_out, b_out, c_out):
    a_out[...] = a[...]
    b_out[...] = b[...]
    c_out[...] = c[...]


def on_device(
    left_factors, mid_factors, row_factors, col_factors, lists, sketch_right, sketch_left, diag_tile
):
    lt = jnp.swapaxes(left_factors, 2, 3).reshape(8, 256, 1024)
    mt = jnp.swapaxes(mid_factors, 2, 3).reshape(8, 256, 1024)
    rt = jnp.swapaxes(row_factors, 1, 2).reshape(256, 1024)
    ct = jnp.swapaxes(col_factors, 1, 2).reshape(256, 1024)
    hbm = pl.BlockSpec(memory_space=pl.ANY)
    vmem = pl.BlockSpec(memory_space=pltpu.VMEM)
    parts = pl.pallas_call(
        kernel,
        out_shape=(
            jax.ShapeDtypeStruct((8, 64, 128), F32),
            jax.ShapeDtypeStruct((8, 8, 1024), F32),
            jax.ShapeDtypeStruct((8, 8, 128), F32),
        ),
        in_specs=[hbm, hbm, hbm, hbm, vmem, hbm, hbm, hbm],
        out_specs=(vmem, vmem, vmem),
        scratch_shapes=[
            pltpu.VMEM((8, 256, 1024), F32),
            pltpu.VMEM((8, 256, 1024), F32),
            pltpu.VMEM((256, 1024), F32),
            pltpu.VMEM((256, 1024), F32),
            pltpu.VMEM((1024, 128), F32),
            pltpu.VMEM((1024, 128), F32),
            pltpu.VMEM((8, 1024, 128), F32),
            pltpu.VMEM((8, 128, 128), F32),
            pltpu.VMEM((UNITS, 16, 64, 128), F32),
            pltpu.VMEM((UNITS, 8, 32, 128), F32),
            pltpu.VMEM((UNITS, 2, 2, 64, 128), F32),
            pltpu.VMEM((UNITS, 2, 2, 2, 64, 128), F32),
            pltpu.VMEM((UNITS, 2, 1, 32, 128), F32),
            pltpu.VMEM((UNITS, 2, 2, 1, 32, 128), F32),
            pltpu.VMEM((2, 1024, 256), BF16),
            pltpu.VMEM((1024, 256), BF16),
            pltpu.VMEM((2, 128, 256), BF16),
            pltpu.VMEM((2, 256, 1024), BF16),
            pltpu.VMEM((2, 256, 1024), BF16),
            pltpu.VMEM((8, 2, 256, 256), BF16),
            pltpu.VMEM((2, 256, 1024), BF16),
            pltpu.VMEM((8, 8, 1024), F32),
            pltpu.SemaphoreType.DMA((24,)),
            pltpu.SemaphoreType.DMA((2, 2)),
            pltpu.SemaphoreType.DMA((2, UNITS, 2)),
            pltpu.SemaphoreType.DMA((16,)),
            pltpu.SemaphoreType.DMA((16,)),
        ],
        compiler_params=pltpu.CompilerParams(
            collective_id=0, has_side_effects=True, vmem_limit_bytes=58 * 1024 * 1024
        ),
        cost_estimate=pl.CostEstimate(
            flops=6_000_000_000, bytes_accessed=21_000_000, transcendentals=0
        ),
    )(lt, mt, rt, ct, lists, sketch_right, sketch_left, diag_tile)
    return pl.pallas_call(
        hand_over,
        out_shape=tuple(jax.ShapeDtypeStruct(p.shape, F32) for p in parts),
        in_specs=[vmem] * 3,
        out_specs=(vmem,) * 3,
        cost_estimate=pl.CostEstimate(flops=0, bytes_accessed=1_200_000, transcendentals=0),
    )(*parts)


def solution(mesh):
    placed = (
        P("target", "inner", None, None),
        P("target", "inner", None, None),
        P("inner", None, None),
        P("inner", None, None),
        P("target", None),
        P(),
        P(),
        P(None, "target"),
    )
    return jax.shard_map(
        on_device,
        mesh=mesh,
        in_specs=placed,
        out_specs=(
            P("target", "inner", None),
            P("target", "inner", None),
            P("target", "inner", None),
        ),
        check_vma=False,
    )
```

```python
import functools

import jax
import jax.numpy as jnp
from jax import lax
from jax.experimental import pallas as pl
from jax.experimental.pallas import tpu as pltpu
from jax.sharding import PartitionSpec as P

F32 = jnp.float32
BF16 = jnp.bfloat16
MESH = pl.DeviceIdType.MESH
NN = ((1,), (0,))
NT = ((1,), (1,))
SIDE = 4
UNITS = 16
LAGS = (3, 6, 9, 12)


def split(value):
    high = value.astype(BF16)
    return high, (value - high.astype(F32)).astype(BF16)


def mm(a, b, dims):
    return lax.dot_general(a, b, (dims, ((), ())), preferred_element_type=F32)


def mm3(a, b, dims):
    return mm(a[0], b[0], dims) + (mm(a[1], b[0], dims) + mm(a[0], b[1], dims))


def mm_top(a, b):
    return lax.dot_general(
        a, b, (NN, ((), ())), precision=lax.Precision.HIGHEST, preferred_element_type=F32
    )


def kernel(
    lt_hbm, mt_hbm, rt_hbm, ct_hbm, lists, om_hbm, psi_hbm, d_hbm,
    left_out, rf_out, core_out,
    lt, mt, rt, ct, om, psi, dfull, dinv, part, half, far1, near1, far2, near2,
    rts, psts, cols, ms, ls, cs, ws, rsf,
    in_sem, send_sem, recv_sem, gs_sem, gr_sem,
):
    inner = lax.axis_index("inner")
    target = lax.axis_index("target")
    z, y = inner // SIDE, lax.rem(inner, SIDE)
    x, core = target // 2, lax.rem(target, 2)

    def turn(v, step):
        return lax.rem(v + step, SIDE)

    z_next = (turn(z, 1) * SIDE + y, turn(z, 3) * SIDE + y)
    y_next = (z * SIDE + turn(y, 1), z * SIDE + turn(y, 3))
    x_next = (turn(x, 1) * 2 + core, turn(x, 3) * 2 + core)
    sibling = x * 2 + (1 - core)

    barrier = pltpu.get_barrier_semaphore()
    for peer in z_next + y_next:
        pl.semaphore_signal(barrier, inc=1, device_id=(peer, target), device_id_type=MESH)
    for peer in x_next + (sibling,):
        pl.semaphore_signal(barrier, inc=1, device_id=(inner, peer), device_id_type=MESH)

    loads = []

    def mt_copy(t):
        return pltpu.make_async_copy(mt_hbm.at[t], mt.at[t], in_sem.at[8 + t])

    def lt_copy(t):
        return pltpu.make_async_copy(lt_hbm.at[t], lt.at[t], in_sem.at[16 + t])

    def load(src, dst):
        copy = pltpu.make_async_copy(src, dst, in_sem.at[len(loads)])
        copy.start()
        loads.append(copy)
        return copy

    rt_load = load(rt_hbm, rt)
    mt_copy(0).start()
    ct_load = load(ct_hbm, ct)
    om_load = load(om_hbm, om)
    lt_copy(0).start()
    psi_load = load(psi_hbm, psi)
    d_load = load(d_hbm, dfull.at[target])

    @pl.loop(1, 8)
    def _(t):
        mt_copy(t).start()
        lt_copy(t).start()

    def g_copy(src, dst, sem, peer):
        return pltpu.make_async_remote_copy(
            src_ref=src, dst_ref=dst, send_sem=gs_sem.at[sem], recv_sem=gr_sem.at[sem],
            device_id=(inner, peer), device_id_type=MESH,
        )

    def x_at(step, which):
        return turn(x, step) * 2 + which

    def gather_first(src, dst, base):
        for sem, peer in ((0, x_next[0]), (1, x_next[1]), (4, sibling)):
            g_copy(src, dst.at[target], base + sem, peer).start()

    def gather_second(dst, base, rows):
        before, after = dst.at[x_at(3, core)], dst.at[x_at(1, core)]
        g_copy(before, before, base + 0, sibling).wait_recv()
        g_copy(after, after, base + 1, sibling).wait_recv()
        low, top = before.at[pl.ds(0, rows)], after.at[pl.ds(rows, rows)]
        g_copy(low, low, base + 2, x_next[0]).start()
        g_copy(top, top, base + 3, x_next[1]).start()
        g_copy(before, before, base + 5, sibling).start()
        g_copy(after, after, base + 6, sibling).start()

    def gather_third(dst, base, rows):
        away = dst.at[x_at(2, core)]
        low, top = away.at[pl.ds(0, rows)], away.at[pl.ds(rows, rows)]
        g_copy(low, low, base + 2, sibling).wait_recv()
        g_copy(top, top, base + 3, sibling).wait_recv()
        g_copy(away, away, base + 7, sibling).start()

    def gather_last(dst, base):
        for sem, step in ((4, 0), (5, 3), (6, 1), (7, 2)):
            block = dst.at[x_at(step, 1 - core)]
            g_copy(block, block, base + sem, sibling).wait_recv()

    def gather_sent(src, dst, base, rows):
        for sem in (0, 1, 4, 5, 6, 7):
            g_copy(dst.at[0], dst.at[0], base + sem, sibling).wait_send()
        for sem in (2, 3):
            piece = dst.at[0, pl.ds(0, rows)]
            g_copy(piece, piece, base + sem, sibling).wait_send()

    def place(u, stage):
        axis = lax.rem(u + stage, 2)
        pos = z + axis * (y - z)
        peers = tuple(a + axis * (b - a) for a, b in zip(z_next, y_next))
        return pos, peers

    bufs = ((part, far1, near1, 2), (half, far2, near2, 1))

    def r_copy(stage, u, sem, src, dst, peer):
        return pltpu.make_async_remote_copy(
            src_ref=src, dst_ref=dst,
            send_sem=send_sem.at[stage, min(sem // 2, 1)], recv_sem=recv_sem.at[stage, u, min(sem // 2, 1)],
            device_id=(peer, target), device_id_type=MESH,
        )

    def piece(stage, u, chunk, h):
        buf, _, _, w = bufs[stage]
        return buf.at[u, pl.ds((2 * chunk + h) * w, w)]

    def start(stage, u):
        pos, peers = place(u, stage)
        _, far, near, _ = bufs[stage]
        for d in (0, 1):
            r_copy(stage, u, d, piece(stage, u, turn(pos, 2), d), far.at[u, d], peers[d]).start()
        for d in (0, 1) if stage == 0 else ():
            r_copy(
                stage, u, 2 + d, piece(stage, u, turn(pos, 1 + 2 * d), 1 - d),
                near.at[u, d, 1 - d], peers[d],
            ).start()

    def middle(stage, u):
        pos, peers = place(u, stage)
        _, far, near, _ = bufs[stage]
        r_copy(stage, u, 0, far.at[u], far.at[u], peers[0]).wait_recv()
        for d in (0, 1):
            own = piece(stage, u, turn(pos, 1 + 2 * d), d)
            own[...] += far[u, d]
            if stage == 0:
                r_copy(stage, u, 4 + d, own, near.at[u, d, d], peers[d]).start()
            else:
                both = half.at[u, pl.ds(2 * turn(pos, 1 + 2 * d), 2)]
                r_copy(stage, u, 4 + d, both, near.at[u, d, :, 0], peers[d]).start()

    def finish(stage, u):
        pos, peers = place(u, stage)
        _, far, near, _ = bufs[stage]
        r_copy(stage, u, 2, near.at[u], near.at[u], peers[0]).wait_recv()
        return [
            piece(stage, u, pos, h)[...] + near[u, 0, h] + near[u, 1, h] for h in (0, 1)
        ]

    def sent(stage):
        _, far, near, _ = bufs[stage]
        r_copy(stage, 0, 0, far, far, z_next[0]).wait_send()
        r_copy(stage, 0, 2, near, near, z_next[0]).wait_send()

    def finish_first(u):
        for h, value in enumerate(finish(0, u)):
            half[u, pl.ds(4 * h, 4)] = value.reshape(4, 32, 128)
        start(1, u)

    def finish_second(u):
        values = [v.reshape(32, 128) for v in finish(1, u)]

        @pl.when(u >= 8)
        def _():
            for h in (0, 1):
                left_out[u - 8, pl.ds(32 * h, 32), :] = values[h]

        @pl.when(u < 8)
        def _():
            for h in (0, 1):
                for m in range(4):
                    rsf[u, :, pl.ds((4 * h + m) * 128, 128)] = values[h][8 * m : 8 * m + 8]

    def within(s):
        return jnp.logical_and(s >= 0, s < UNITS)

    def service(s):
        a, b, c, d = LAGS
        pl.when(within(s - a))(lambda: middle(0, s - a))
        pl.when(within(s - b))(lambda: finish_first(s - b))
        pl.when(within(s - c))(lambda: middle(1, s - c))
        pl.when(within(s - d))(lambda: finish_second(s - d))

    def chunk_at(u, zz, yy):
        axis = lax.rem(u, 2)
        first, second = zz + axis * (yy - zz), yy + axis * (zz - yy)
        return first * SIDE + second

    def put(ref, value):
        ref[0], ref[1] = split(value)

    def got(ref):
        return ref[0], ref[1]

    rt_load.wait()
    for p in (0, 1):
        pair = split(rt[pl.ds(128 * p, 128), :].T)
        rts[p, :, pl.ds(0, 128)], rts[p, :, pl.ds(128, 128)] = pair
    ct_load.wait()
    om_load.wait()
    put(ws, ct[...])
    put(cols, mm3(got(ws), split(om[...]), NN).T)

    row_tile = lax.broadcasted_iota(jnp.int32, (128, 128), 0) // 64
    col_tile = lax.broadcasted_iota(jnp.int32, (128, 128), 1) // 64
    tile_ids = inner * 4 + lax.broadcasted_iota(jnp.int32, (128, 1), 0) // 64
    cs[...] = jnp.zeros_like(cs)

    def right_unit(t):
        mt_copy(t).wait()
        put(ms, mt[t])
        for p in (0, 1):
            cut = pl.ds(128 * p, 128)
            both = mm(ms[0, cut, :], rts[p], NN)
            coupling = both[:, :128] + (
                both[:, 128:] + mm(ms[1, cut, :], rts[p, :, pl.ds(0, 128)], NN)
            )
            present = jnp.sum(
                (lists[pl.ds(t, 1), :] == tile_ids + 2 * p).astype(F32), axis=1, keepdims=True
            )
            coupling = jnp.where(row_tile == col_tile, coupling, 0.0) * present
            cs[t, 0, cut, cut], cs[t, 1, cut, cut] = split(coupling)
        lt_copy(t).wait()
        put(ls, lt[t])
        both = mm(ls[0], psts[...], NN)
        projected = both[:, :128] + (both[:, 128:] + mm(ls[1], psts[:, pl.ds(0, 128)], NN))
        joined = split(mm3(split(projected.T), got(cs.at[t]), NN))
        for n in range(4):
            cut = pl.ds(256 * n, 256)
            block = mm3(joined, (ws[0, :, cut], ws[1, :, cut]), NN)
            for m in (0, 1):
                value = block[:, 128 * m : 128 * m + 128].reshape(16, 8, 128)
                for i in range(16):
                    part[t, chunk_at(t, i // 4, i % 4), pl.ds((2 * n + m) * 8, 8), :] = value[i]

    def left_unit(t):
        u = t + 8
        inner_left = split(mm3(got(cols), got(cs.at[t]), NT))
        put(ls, lt[t])
        for zz in range(4):
            cut = pl.ds(256 * zz, 256)
            block = mm3(inner_left, (ls[0, :, cut], ls[1, :, cut]), NN).T
            for yy in range(4):
                part[u, chunk_at(u, zz, yy)] = block[64 * yy : 64 * yy + 64]

    def own_inverse():
        d_load.wait()
        block = dfull[target, pl.ds(pl.multiple_of(target * 128, 128), 128), :]
        rows = lax.broadcasted_iota(jnp.int32, (128, 128), 0)
        lanes = lax.broadcasted_iota(jnp.int32, (128, 128), 1)
        eye = (rows == lanes).astype(F32)
        diagonal = jnp.where(rows == lanes, block, 0.0)
        power = eye - block / jnp.sum(diagonal, axis=1, keepdims=True)
        product = eye + power
        for _ in range(6):
            power = mm_top(power, power)
            product = product + mm_top(product, power)
        dinv[target] = product / jnp.sum(diagonal, axis=0, keepdims=True)

    def solve_step(j):
        cut = pl.ds(128 * j, 128)
        rhs = rsf[:, :, cut].reshape(64, 128)
        if j > 0:
            before = pl.ds(0, 128 * j)
            earlier = rf_out[:, :, before].reshape(64, 128 * j)
            rhs = rhs - mm3(split(earlier), split(dfull[j, before, :]), NN)
        rf_out[:, :, cut] = mm3(split(rhs), split(dinv[j]), NN).reshape(8, 8, 128)

    psi_load.wait()
    psts[:, pl.ds(0, 128)], psts[:, pl.ds(128, 128)] = split(psi[...])
    right_unit(0)
    pl.semaphore_wait(barrier, 7)
    start(0, 0)
    gather_first(d_hbm, dfull, 0)

    @pl.loop(1, 8)
    def _(s):
        right_unit(s)
        start(0, s)
        service(s)

    @pl.loop(8, 16)
    def _(s):
        left_unit(s - 8)
        start(0, s)

        @pl.when(s == 9)
        def _():
            own_inverse()
            gather_first(dinv.at[target], dinv, 8)

        @pl.when(s == 12)
        def _():
            gather_second(dfull, 0, 512)
            gather_second(dinv, 8, 64)

        @pl.when(s == 15)
        def _():
            gather_third(dfull, 0, 512)
            gather_third(dinv, 8, 64)

        service(s)

    solve_from = max(16, 8 + LAGS[3])

    @pl.loop(16, solve_from)
    def _(s):
        service(s)

    gather_last(dfull, 0)
    gather_last(dinv, 8)
    for j in range(8):
        solve_step(j)
        if j % 2:
            service(solve_from + j // 2)
    core_out[...] = mm3(
        split(rsf[...].reshape(64, 1024)), split(om[...]), NN
    ).reshape(8, 8, 128)

    @pl.loop(solve_from + 4, 16 + LAGS[3])
    def _(s):
        service(s)

    gather_sent(d_hbm, dfull, 0, 512)
    gather_sent(dinv, dinv, 8, 64)

    sent(0)
    sent(1)


def hand_over(a, b, c, a_out, b_out, c_out):
    a_out[...] = a[...]
    b_out[...] = b[...]
    c_out[...] = c[...]


def on_device(
    left_factors, mid_factors, row_factors, col_factors, lists, sketch_right, sketch_left, diag_tile
):
    lt = jnp.swapaxes(left_factors, 2, 3).reshape(8, 256, 1024)
    mt = jnp.swapaxes(mid_factors, 2, 3).reshape(8, 256, 1024)
    rt = jnp.swapaxes(row_factors, 1, 2).reshape(256, 1024)
    ct = jnp.swapaxes(col_factors, 1, 2).reshape(256, 1024)
    hbm = pl.BlockSpec(memory_space=pl.ANY)
    vmem = pl.BlockSpec(memory_space=pltpu.VMEM)
    parts = pl.pallas_call(
        kernel,
        out_shape=(
            jax.ShapeDtypeStruct((8, 64, 128), F32),
            jax.ShapeDtypeStruct((8, 8, 1024), F32),
            jax.ShapeDtypeStruct((8, 8, 128), F32),
        ),
        in_specs=[hbm, hbm, hbm, hbm, vmem, hbm, hbm, hbm],
        out_specs=(vmem, vmem, vmem),
        scratch_shapes=[
            pltpu.VMEM((8, 256, 1024), F32),
            pltpu.VMEM((8, 256, 1024), F32),
            pltpu.VMEM((256, 1024), F32),
            pltpu.VMEM((256, 1024), F32),
            pltpu.VMEM((1024, 128), F32),
            pltpu.VMEM((1024, 128), F32),
            pltpu.VMEM((8, 1024, 128), F32),
            pltpu.VMEM((8, 128, 128), F32),
            pltpu.VMEM((UNITS, 16, 64, 128), F32),
            pltpu.VMEM((UNITS, 8, 32, 128), F32),
            pltpu.VMEM((UNITS, 2, 2, 64, 128), F32),
            pltpu.VMEM((UNITS, 2, 2, 2, 64, 128), F32),
            pltpu.VMEM((UNITS, 2, 1, 32, 128), F32),
            pltpu.VMEM((UNITS, 2, 2, 1, 32, 128), F32),
            pltpu.VMEM((2, 1024, 256), BF16),
            pltpu.VMEM((1024, 256), BF16),
            pltpu.VMEM((2, 128, 256), BF16),
            pltpu.VMEM((2, 256, 1024), BF16),
            pltpu.VMEM((2, 256, 1024), BF16),
            pltpu.VMEM((8, 2, 256, 256), BF16),
            pltpu.VMEM((2, 256, 1024), BF16),
            pltpu.VMEM((8, 8, 1024), F32),
            pltpu.SemaphoreType.DMA((24,)),
            pltpu.SemaphoreType.DMA((2, 2)),
            pltpu.SemaphoreType.DMA((2, UNITS, 2)),
            pltpu.SemaphoreType.DMA((16,)),
            pltpu.SemaphoreType.DMA((16,)),
        ],
        compiler_params=pltpu.CompilerParams(
            collective_id=0, has_side_effects=True, vmem_limit_bytes=58 * 1024 * 1024
        ),
        cost_estimate=pl.CostEstimate(
            flops=6_000_000_000, bytes_accessed=21_000_000, transcendentals=0
        ),
    )(lt, mt, rt, ct, lists, sketch_right, sketch_left, diag_tile)
    return pl.pallas_call(
        hand_over,
        out_shape=tuple(jax.ShapeDtypeStruct(p.shape, F32) for p in parts),
        in_specs=[vmem] * 3,
        out_specs=(vmem,) * 3,
        cost_estimate=pl.CostEstimate(flops=0, bytes_accessed=1_200_000, transcendentals=0),
    )(*parts)


def solution(mesh):
    placed = (
        P("target", "inner", None, None),
        P("target", "inner", None, None),
        P("inner", None, None),
        P("inner", None, None),
        P("target", None),
        P(),
        P(),
        P(None, "target"),
    )
    return jax.shard_map(
        on_device,
        mesh=mesh,
        in_specs=placed,
        out_specs=(
            P("target", "inner", None),
            P("target", "inner", None),
            P("target", "inner", None),
        ),
        check_vma=False,
    )
```
